32 devices in a mesh: groups: 2 (over y), feat: 8 (over z, x), pair: 2 (over core).
Axes of the slice: x: 2, y: 2, z: 4, core: 2. Of those that a mesh axis runs over, the one named last changes fastest.
Arguments:
- codes: bfloat16 [2048, 2, 8192], P(('groups', 'feat')), parts along dimension 0, may hold values from 0 to 2
- block_ids: int32 [2048, 2], P(('groups', 'feat')), parts along dimension 0, may hold values from 0 to 3, all different within a row; in each aligned block of 128 rows (0 to 127, 128 to 255, ...) at most 128 rows name the same one
- decoder: bfloat16 [65536, 4096], P('feat', 'pair'), may hold values from -0.046875 to 0.046875
- targets: bfloat16 [2048, 2, 4096], P(('groups', 'feat'), None, 'pair'), parts along dimension 0, may hold values from -6 to 6
Outputs:
- reconstruction: bfloat16 [2048, 2, 4096], P(('groups', 'feat'), None, 'pair'), parts along dimension 0
- code_grad: bfloat16 [2048, 2, 8192], P(('groups', 'feat')), parts along dimension 0
- weight_grad: bfloat16 [131072, 4096], P(('groups', 'feat'), 'pair'), parts along dimension 0
The draws below stay inside these ranges and needn't reach their ends.
There are 2 independent parts, one for each index of `groups`. The reference program is written for one: setup_inputs(seed, part) draws one part's arguments, and reference() takes and returns one part's arrays. A program takes and returns all parts, laid end to end along the dimension named above; an argument that names none is the same for every part. Nothing has to cross between parts.
Inputs may be any that keep to these rules, and one draw needn't show every extreme that they name: `block_ids`: each token names 2 different blocks. The 128 tokens of one index of feat name one block at most 128 times, and in every draw some block is named exactly 128 times by the tokens of some index.
All inputs are finite; a program needn't handle non-finite values.
Results may differ from the reference program's by a relative error of at most 0.006.
Values may be sent and summed in bfloat16 or wider, within the bound.
No kernel may reach another device: no remote copies, remote signals or barrier semaphores. Data moves between devices by JAX's collectives and lax.ppermute only.
A program may use at most 256 MiB of HBM per device.

```python
import math
import jax
import jax.numpy as jnp
import numpy as np
from jax import lax

D = 4096
F = 32768
PAIRS = 2
ACTIVE = 2
TOK_DEV = 128
BLOCKS = 4
BLOCK = 8192
CAPACITY = 128
TOKENS = 1024
N_FEAT = 8


def shard_levels(key, shape, pieces, low, high):
    gain, own = 1.0, jax.random.fold_in(key, 6)
    for dim, parts in pieces:
        heights = jnp.exp(jax.random.uniform(jax.random.fold_in(own, dim), (parts,), jnp.float32, low / len(pieces), high / len(pieces)))
        gain = gain * jnp.repeat(heights, shape[dim] // parts).reshape([-1 if axis == dim else 1 for axis in range(len(shape))])
    return gain


def shared_out(stream_key, own, number, rows, count, top, limit, slope):
    sequence = jax.random.permutation(stream_key, count)
    packed, common = load_shares(count, rows * top, limit, slope, True), load_shares(count, rows * top, limit, slope, False)
    places = jnp.arange(count)

    def named(tallies, offset_by):
        used = int((tallies > 0).sum())
        fixed = max(1, used // 4)
        passed = fixed + (places - fixed + offset_by * (used - fixed)) % max(1, count - fixed)
        return jnp.zeros((count,), jnp.int32).at[sequence[jnp.where(places < fixed, places, passed)]].set(jnp.asarray(tallies, jnp.int32))

    tallies = jnp.where(number % 4 == 0, named(packed, number // 4), named(common, number - number // 4 - 1))
    mixed = jax.random.permutation(jax.random.fold_in(own, 3), count)
    source_of, sink = mixed[0:count // 2 * 2:2], mixed[1:count // 2 * 2:2]
    room = jnp.minimum(tallies[source_of] - 1, limit - tallies[sink]) // 2
    room = jnp.where((source_of == sequence[0]) | (sink == sequence[0]) | (tallies[sink] == 0), 0, jnp.maximum(room, 0))
    passed = jax.random.randint(jax.random.fold_in(own, 4), (count // 2,), 0, 1 << 20) % (room + 1)
    tallies = tallies.at[source_of].add(-passed).at[sink].add(passed)
    items = jnp.searchsorted(jnp.cumsum(tallies), jnp.arange(rows * top), side="right").astype(jnp.int32)
    grid = items.reshape(top, rows).T
    grid = grid[jax.random.permutation(jax.random.fold_in(own, 1), rows)]
    offset_by = jax.random.randint(jax.random.fold_in(own, 2), (rows, 1), 0, top)
    return jnp.take_along_axis(grid, (jnp.arange(top)[None, :] + offset_by) % top, axis=1)


def load_shares(count, total, reach, skew, full):
    weights = [(1 << 20) // math.isqrt(rank ** skew) + 1 for rank in range(1, count + 1)]
    largest = reach if full else min(reach, max(-(-total // count), total * weights[0] // sum(weights)))
    least = 1 if total - largest >= count - 1 else 0
    given, surplus = [largest] + [least] * (count - 1), total - largest - least * (count - 1)
    while surplus > 0:
        movable = [i for i in range(1, count) if given[i] < largest] or [i for i in range(1, count) if given[i] < reach]
        mass, budget = sum([weights[i] for i in movable]), surplus
        for i in movable:
            addition = min(reach - given[i], max(1, budget * weights[i] // mass), surplus)
            given[i] = given[i] + addition
            surplus = surplus - addition
    return np.array(given)


def gaussian(key, dims, scale, bound, pieces=(), kind=jnp.bfloat16):
    array = jax.random.normal(key, dims, jnp.float32) * scale
    if len(pieces) > 0:
        array = shard_levels(key, dims, pieces, -0.22, 0.18) * array
    return jnp.clip(array, min=-bound, max=bound).astype(kind)


def setup_inputs(seed: int = 0, part: int = 0) -> dict:
    seeds = jax.random.split(jax.random.key(seed), 5)
    part_keys = jax.random.split(jax.random.fold_in(seeds[4], part), 5)
    codes = jnp.clip(2.0 * jax.random.uniform(part_keys[0], (TOKENS, ACTIVE, BLOCK), jnp.float32) ** shard_levels(part_keys[0], (TOKENS, ACTIVE, BLOCK), ((0, 8),), -0.2, 0.2), 0.0, 2.0).astype(jnp.bfloat16)
    block_ids_keys = jax.random.split(jax.random.fold_in(part_keys[1], 1), TOKENS // TOK_DEV)
    block_ids_turns = jax.random.permutation(jax.random.fold_in(part_keys[1], 3), TOKENS // TOK_DEV)
    block_ids = jax.vmap(lambda own, number: shared_out(jax.random.fold_in(part_keys[1], 2), own, number, TOK_DEV, BLOCKS, ACTIVE, CAPACITY, 2))(block_ids_keys, block_ids_turns).reshape((TOKENS, ACTIVE))
    decoder = gaussian(seeds[2], (PAIRS * F, D), (ACTIVE * BLOCK) ** -0.5, 0.046875, ((0, 8), (1, 2)))
    targets = gaussian(part_keys[3], (TOKENS, PAIRS, D), 1.0, 6.0, ((0, 8), (2, 2)))
    return {"codes": codes, "block_ids": block_ids, "decoder": decoder, "targets": targets}


error_scale = 0.125


def reference(codes, block_ids, decoder, targets):
    tok_rows, per_token, block_width = codes.shape
    entries = tok_rows * per_token
    capall = N_FEAT * CAPACITY
    flat_ids = block_ids.reshape(-1).astype(jnp.int32)
    flat_codes = codes.reshape(entries, block_width)
    entry_token = jnp.arange(entries, dtype=jnp.int32) // per_token

    def select_block(block_id):
        entry_index = jnp.nonzero(flat_ids == block_id, size=capall, fill_value=entries)[0].astype(jnp.int32)
        is_live = entry_index < entries
        clipped = jnp.minimum(entry_index, entries - 1).astype(jnp.int32)
        picked = jnp.where(is_live[:, None], flat_codes[clipped], jnp.zeros_like(flat_codes[clipped]))
        return is_live, clipped, picked

    def weights_of(block_id, target):
        start = (target * F + block_id * BLOCK).astype(jnp.int32)
        return lax.dynamic_slice_in_dim(decoder, start, BLOCK, 0)

    def forward_step(rebuilt, block_id):
        is_live, clipped, picked = select_block(block_id)
        token_index = entry_token[clipped]
        for target in range(PAIRS):
            partial_value = jnp.dot(picked, weights_of(block_id, target), preferred_element_type=jnp.float32)
            partial_value = lax.optimization_barrier(partial_value.astype(jnp.bfloat16)).astype(jnp.float32)
            partial_value = jnp.where(is_live[:, None], partial_value, jnp.zeros_like(partial_value))
            rebuilt = rebuilt.at[token_index, target].add(partial_value)
        return rebuilt, None

    block_range = jnp.arange(BLOCKS, dtype=jnp.int32)
    rebuilt, _ = lax.scan(forward_step, jnp.zeros((tok_rows, PAIRS, D), jnp.float32), block_range)
    error_grad = ((rebuilt - targets.astype(jnp.float32)) * error_scale).astype(jnp.bfloat16)

    def backward_step(code_total, block_id):
        is_live, clipped, picked = select_block(block_id)
        token_index = entry_token[clipped]
        weight_parts = []
        for target in range(PAIRS):
            grad_rows = error_grad[token_index, target]
            grad_rows = jnp.where(is_live[:, None], grad_rows, jnp.zeros_like(grad_rows))
            weights = weights_of(block_id, target)
            weight_part = lax.dot_general(picked, grad_rows, (((0,), (0,)), ((), ())), preferred_element_type=jnp.float32)
            weight_parts.append(weight_part.astype(jnp.bfloat16))
            code_term = lax.dot_general(grad_rows, weights, (((1,), (1,)), ((), ())), preferred_element_type=jnp.float32)
            code_term = lax.optimization_barrier(code_term.astype(jnp.bfloat16)).astype(jnp.float32)
            code_term = jnp.where(is_live[:, None], code_term, jnp.zeros_like(code_term))
            code_total = code_total.at[clipped].add(code_term)
        return code_total, jnp.stack(weight_parts)

    code_total, block_grads = lax.scan(backward_step, jnp.zeros((entries, block_width), jnp.float32), block_range)
    weight_grad = jnp.transpose(block_grads, (1, 0, 2, 3)).reshape(PAIRS * F, D)
    code_grad = code_total.astype(jnp.bfloat16).reshape(tok_rows, per_token, block_width)
    return rebuilt.astype(jnp.bfloat16), code_grad, weight_grad
```

```python
import jax
import jax.numpy as jnp
from jax import lax
from jax.experimental import pallas as pl
from jax.experimental.pallas import tpu as pltpu
from jax.sharding import PartitionSpec as P

PAIRS = 2
SPLIT = (1, 1)
STRIP = 1024
VMEM_LIMIT = 48 * 1024 * 1024


error_scale = 0.125


def slotted(codes, block_ids, decoder, targets):
    tok_rows, per_token, block_width = codes.shape
    half_width = decoder.shape[1]
    owners = lax.axis_size("feat")
    blocks = owners // PAIRS
    capacity = 2 * tok_rows * per_token // blocks
    flat_ids = block_ids.reshape(-1)
    matches = (flat_ids[:, None] == jnp.arange(blocks, dtype=jnp.int32)[None, :]).astype(jnp.int32)
    ranking = jnp.sum((jnp.cumsum(matches, axis=0) - 1) * matches, axis=1)
    slot_lists = [(target * blocks + flat_ids) * capacity + ranking for target in range(PAIRS)]
    values = codes.reshape(-1, block_width)
    outgoing = jnp.zeros((owners * capacity, values.shape[1]), jnp.bfloat16)
    for slot_index in slot_lists:
        outgoing = outgoing.at[slot_index].set(values)
    outgoing = outgoing.reshape(owners, capacity, values.shape[1])
    arrived = lax.all_to_all(outgoing, "feat", split_axis=0, concat_axis=0, tiled=True)
    partial_rows = jnp.einsum("snb,bd->snd", arrived, decoder, preferred_element_type=jnp.float32)
    sent_back = lax.all_to_all(
        partial_rows.astype(jnp.bfloat16), "feat", split_axis=0, concat_axis=0, tiled=True
    )
    returned_flat = sent_back.reshape(owners * capacity, half_width)
    rebuilt = jnp.stack(
        [
            jnp.sum(
                returned_flat[slot_index]
                .astype(jnp.float32)
                .reshape(tok_rows, per_token, half_width),
                axis=1,
            )
            for slot_index in slot_lists
        ],
        axis=1,
    )
    error_grad = ((rebuilt - targets.astype(jnp.float32)) * error_scale).astype(jnp.bfloat16)
    grad_out = jnp.zeros((owners * capacity, half_width), jnp.bfloat16)
    for target in range(PAIRS):
        grad_out = grad_out.at[slot_lists[target]].set(
            jnp.repeat(error_grad[:, target], per_token, axis=0)
        )
    grad_out = grad_out.reshape(owners, capacity, half_width)
    arrived_grad = lax.all_to_all(grad_out, "feat", split_axis=0, concat_axis=0, tiled=True)
    summed = jnp.einsum("snd,bd->snb", arrived_grad, decoder, preferred_element_type=jnp.float32)
    summed = lax.psum(summed, "pair")
    sent_back = lax.all_to_all(
        summed.astype(jnp.bfloat16), "feat", split_axis=0, concat_axis=0, tiled=True
    )
    weight_grad = lax.dot_general(
        arrived.reshape(-1, block_width),
        arrived_grad.reshape(-1, half_width),
        (((0,), (0,)), ((), ())),
        preferred_element_type=jnp.float32,
    ).astype(jnp.bfloat16)
    code_flat = sent_back.reshape(owners * capacity, sent_back.shape[2])
    code_total = code_flat[slot_lists[0]].astype(jnp.float32)
    for slot_index in slot_lists[1:]:
        code_total = code_total + code_flat[slot_index].astype(jnp.float32)
    code_grad = code_total.astype(jnp.bfloat16).reshape(tok_rows, per_token, sent_back.shape[2])
    return (rebuilt.astype(jnp.bfloat16), code_grad, weight_grad)


def add(*terms):
    return sum(term.astype(jnp.float32) for term in terms).astype(jnp.bfloat16)


def call(kernel, core, operands, specs, grid, outs, out_specs, scratch, flops, moved, alias={}):
    return pl.pallas_call(
        kernel,
        grid_spec=pltpu.PrefetchScalarGridSpec(
            num_scalar_prefetch=1,
            grid=(grid,),
            in_specs=specs,
            out_specs=out_specs,
            scratch_shapes=scratch,
        ),
        out_shape=outs,
        input_output_aliases=alias,
        compiler_params=pltpu.CompilerParams(
            vmem_limit_bytes=VMEM_LIMIT, dimension_semantics=("arbitrary",)
        ),
        cost_estimate=pl.CostEstimate(flops=flops, bytes_accessed=moved, transcendentals=0),
    )(core, *operands)


def rebuild(core, own, other, decoder):
    rows, half = own.shape
    depth = decoder.shape[1]
    strips = half // min(STRIP, half)
    kept = rows // 2

    def kernel(core_ref, own_ref, other_ref, decoder_ref, *rest):
        upper_ref, lower_ref, total = rest[-3:]
        step = pl.program_id(0)

        @pl.when(step == 0)
        def _():
            total[...] = jnp.zeros_like(total)

        @pl.when(step < strips)
        def _():
            total[...] += jnp.dot(
                own_ref[...], decoder_ref[...], preferred_element_type=jnp.float32
            )

        @pl.when(step >= strips)
        def _():
            total[...] += jnp.dot(
                other_ref[...], decoder_ref[...], preferred_element_type=jnp.float32
            )

        @pl.when(step == 2 * strips - 1)
        def _():
            upper_ref[...] = total[:kept].astype(jnp.bfloat16)
            lower_ref[...] = total[kept:].astype(jnp.bfloat16)

    def strip(step, core_ref):
        side = jnp.where(step < strips, core_ref[0], 1 - core_ref[0])
        return side * strips + lax.rem(step, strips), 0

    out = jax.ShapeDtypeStruct((kept, depth), jnp.bfloat16)
    return call(
        kernel,
        core,
        [own, other, decoder],
        [
            pl.BlockSpec((rows, STRIP), lambda i, c: (0, jnp.minimum(i, strips - 1))),
            pl.BlockSpec((rows, STRIP), lambda i, c: (0, jnp.maximum(i - strips, 0))),
            pl.BlockSpec((STRIP, depth), strip),
        ],
        2 * strips,
        [out, out],
        [pl.BlockSpec((kept, depth), lambda i, c: (0, 0))] * 2,
        [pltpu.VMEM((rows, depth), jnp.float32)],
        4 * rows * half * depth,
        4 * half * depth,
    )


def code_terms(core, upper, lower, decoder):
    kept, depth = upper.shape
    half = decoder.shape[0] // 2
    strips = half // min(STRIP, half)
    rows = 2 * kept

    def kernel(core_ref, upper_ref, lower_ref, decoder_ref, give_ref, keep_ref, grads):
        step = pl.program_id(0)

        @pl.when(step == 0)
        def _():
            grads[:kept, :] = upper_ref[...]
            grads[kept:, :] = lower_ref[...]

        product = lax.dot_general(
            grads[...],
            decoder_ref[...],
            (((1,), (1,)), ((), ())),
            preferred_element_type=jnp.float32,
        ).astype(jnp.bfloat16)

        @pl.when(step < strips)
        def _():
            give_ref[...] = product

        @pl.when(step >= strips)
        def _():
            keep_ref[...] = product

    def strip(step, core_ref):
        side = jnp.where(step < strips, 1 - core_ref[0], core_ref[0])
        return side * strips + lax.rem(step, strips), 0

    out = jax.ShapeDtypeStruct((rows, half), jnp.bfloat16)
    return call(
        kernel,
        core,
        [upper, lower, decoder],
        [pl.BlockSpec((kept, depth), lambda i, c: (0, 0))] * 2
        + [pl.BlockSpec((STRIP, depth), strip)],
        2 * strips,
        [out, out],
        [
            pl.BlockSpec((rows, STRIP), lambda i, c: (0, jnp.minimum(i, strips - 1))),
            pl.BlockSpec((rows, STRIP), lambda i, c: (0, jnp.maximum(i - strips, 0))),
        ],
        [pltpu.VMEM((rows, depth), jnp.bfloat16)],
        4 * rows * half * depth,
        4 * half * depth,
    )


def weight_half(side, rows, grads, base=None):
    half = rows[0].shape[1]
    depth = grads[0].shape[1]
    strips = half // min(STRIP, half)
    sizes = [piece.shape[0] for piece in grads]
    total = sum(sizes)
    pieces = len(rows)

    def kernel(side_ref, *refs):
        row_refs, grad_refs = refs[:pieces], refs[pieces : pieces + len(grads)]
        out_ref, stacked = refs[-2:]

        @pl.when(pl.program_id(0) == 0)
        def _():
            at = 0
            for size, ref in zip(sizes, grad_refs):
                stacked[at : at + size, :] = ref[...]
                at += size

        left = jnp.concatenate([ref[...] for ref in row_refs], axis=0)
        out_ref[...] = lax.dot_general(
            left, stacked[...], (((0,), (0,)), ((), ())), preferred_element_type=jnp.float32
        ).astype(jnp.bfloat16)

    operands = rows + grads
    specs = [pl.BlockSpec((piece.shape[0], STRIP), lambda i, c: (0, i)) for piece in rows]
    specs += [pl.BlockSpec(piece.shape, lambda i, c: (0, 0)) for piece in grads]
    alias = {}
    if base is not None:
        alias = {1 + len(operands): 0}
        operands = operands + [base]
        specs = specs + [pl.BlockSpec(memory_space=pl.ANY)]
    return call(
        kernel,
        side,
        operands,
        specs,
        strips,
        jax.ShapeDtypeStruct((2 * half, depth), jnp.bfloat16),
        pl.BlockSpec((STRIP, depth), lambda i, c: (c[0] * strips + i, 0)),
        [pltpu.VMEM((total, depth), jnp.bfloat16)],
        2 * total * half * depth,
        2 * half * (depth + total),
        alias,
    )


NEAR, FAR = 0, 1


class Bag:
    def __init__(self):
        self.heres, self.theres, self.waits, self.ys = ([None, None] for _ in range(4))


def dense(codes, block_ids, decoder, targets):
    tok_rows, per_token, width = codes.shape
    half = width // 2
    me = lax.axis_index("feat")
    core = lax.axis_index("pair")
    core_at = core.astype(jnp.int32).reshape(1)
    layer = me // 2
    target = layer // 2
    inner = (layer == 1) | (layer == 2)
    block = me % 4
    sibling = block ^ 1
    unit = tok_rows // sum(SPLIT)
    starts = (0, SPLIT[0] * unit)
    counts = (SPLIT[0] * unit, tok_rows - SPLIT[0] * unit)

    def over_layers(pairs):
        return [(a * 2 + x, b * 2 + x) for a, b in pairs for x in range(2)]

    def feat(value, perm):
        return lax.ppermute(value, "feat", perm)

    NEIGHBOUR = over_layers([(0, 1), (1, 0), (2, 3), (3, 2)])
    MIDDLE = over_layers([(1, 2), (2, 1)])
    OUTWARD = over_layers([(1, 0), (2, 3)])
    INWARD = over_layers([(0, 1), (3, 2)])
    MIRROR = over_layers([(0, 3), (3, 0), (1, 2), (2, 1)])
    ACROSS = over_layers([(0, 2), (2, 0), (1, 3), (3, 1)])
    COLUMN = [(i, i ^ 1) for i in range(8)]

    def other_core(value):
        return lax.ppermute(value, "pair", [(0, 1), (1, 0)])

    def pick(value, ids, wanted):
        hits = (ids == wanted)[:, :, None]
        return jnp.where(hits[:, 0], value[0], jnp.where(hits[:, 1], value[1], 0))

    def stack(*values):
        return jnp.concatenate(values, axis=0)

    def part_of(value, i):
        return value[starts[i] : starts[i] + counts[i]]

    def error(rebuilt, wanted):
        gap = rebuilt.astype(jnp.float32) - wanted.astype(jnp.float32)
        return (gap * error_scale).astype(jnp.bfloat16)

    parts = (Bag(), Bag())
    kinds = tuple((Bag(), Bag()) for kind in (NEAR, FAR))
    token = []

    def gate(*values):
        out = lax.optimization_barrier((*values, *token))[: len(values)]
        return out[0] if len(values) == 1 else out

    def done(*values):
        token[:] = values

    def prep(i):
        source = codes if i == 0 else gate(codes)
        own = lax.dynamic_slice(source, (starts[i], 0, core * half), (counts[i], per_token, half))
        own = jnp.swapaxes(own, 0, 1)
        parts[i].own = own
        if i == 0:
            parts[i].near = feat(own, NEIGHBOUR)
            parts[i].mid = feat(own, MIDDLE)
        done(own)

    def ids(i):
        parts[i].near, parts[i].mid, mine = gate(parts[i].near, parts[i].mid, block_ids)
        near, mirror, across = feat(mine, NEIGHBOUR), feat(mine, MIRROR), feat(mine, ACROSS)
        parts[0].slots = [
            block_ids,
            near,
            jnp.where(inner, mirror, across),
            jnp.where(inner, across, mirror),
        ]
        done(mine)

    def aims(i):
        wanted = part_of(gate(targets), i)
        kinds[NEAR][i].aim = lax.dynamic_index_in_dim(wanted, target, 1, keepdims=False)
        far = lax.dynamic_index_in_dim(wanted, 1 - target, 1, keepdims=False)
        kinds[FAR][i].aim = feat(far, MIRROR)
        done(far, kinds[NEAR][i].aim)

    def named(i, slot):
        return part_of(parts[0].slots[slot], i)

    def in1(i):
        near, mid = gate(parts[i].near, parts[i].mid)
        parts[i].in_end = feat(mid, OUTWARD)
        parts[i].out_mid = feat(near, MIDDLE)
        parts[i].near, parts[i].mid = near, mid
        done(near, mid)

    def in1x(i):
        own, near = gate(parts[i].own, parts[i].near)
        a, b = named(i, 0), named(i, 1)
        crossing = stack(pick(own, a, sibling), pick(near, b, sibling))
        kinds[NEAR][i].crossed = feat(crossing, COLUMN)
        kinds[NEAR][i].kept = stack(pick(own, a, block), pick(near, b, block))
        done(crossing, kinds[NEAR][i].kept)

    def in2(i):
        in_end, out_mid, mid = gate(parts[i].in_end, parts[i].out_mid, parts[i].mid)
        parts[i].out_end = feat(out_mid, OUTWARD)
        parts[i].out_mid = out_mid
        if i == 0:
            parts[1].mid = feat(gate(parts[1].own), MIDDLE)
        far_in = jnp.where(inner, mid, in_end)
        crossing = pick(far_in, named(i, 2), sibling)
        parts[i].in_crossed = feat(crossing, COLUMN)
        parts[i].in_kept = pick(far_in, named(i, 2), block)
        done(crossing, parts[i].in_kept)

    def in3(i):
        kept, crossed = gate(kinds[NEAR][i].kept, kinds[NEAR][i].crossed)
        rows = stack(kept, crossed)
        kinds[NEAR][i].rows = rows
        kinds[NEAR][i].rows_other = other_core(rows)
        done(rows)

    def in4(i):
        out_end, out_mid = gate(parts[i].out_end, parts[i].out_mid)
        if i == 0:
            parts[1].near = feat(gate(parts[1].own), NEIGHBOUR)
        far_out = jnp.where(inner, out_mid, out_end)
        crossing = pick(far_out, named(i, 3), sibling)
        parts[i].out_crossed = feat(crossing, COLUMN)
        parts[i].out_kept = pick(far_out, named(i, 3), block)
        done(crossing, parts[i].out_kept)

    def in5(i):
        rows = stack(*gate(parts[i].in_kept, parts[i].out_kept, parts[i].in_crossed, parts[i].out_crossed))
        kinds[FAR][i].rows = rows
        kinds[FAR][i].rows_other = other_core(rows)
        done(rows)

    def sums(kind):
        def step(i):
            own, other = gate(kinds[kind][i].rows, kinds[kind][i].rows_other)
            upper, lower = rebuild(core_at, own, other, decoder)
            kinds[kind][i].rows, kinds[kind][i].rows_other = own, other
            kinds[kind][i].upper = upper
            kinds[kind][i].lower = feat(lower, COLUMN)
            done(upper, lower)

        return step

    def err1(kind):
        def step(i):
            total = add(*gate(kinds[kind][i].upper, kinds[kind][i].lower))
            first, second = total[: counts[i]], total[counts[i] :]
            keep, send = first, second
            if kind == FAR:
                keep, send = jnp.where(inner, first, second), jnp.where(inner, second, first)
            kinds[kind][i].keep = keep
            kinds[kind][i].sent = feat(send, NEIGHBOUR)
            done(keep, send)

        return step

    def err2(kind):
        def step(i):
            rebuilt = add(*gate(kinds[kind][i].keep, kinds[kind][i].sent))
            grad = error(rebuilt, gate(kinds[kind][i].aim))
            kinds[kind][i].rebuilt = rebuilt
            kinds[kind][i].grad = grad
            kinds[kind][i].grad_sent = feat(grad, NEIGHBOUR)
            done(grad)

        return step

    def err3(kind):
        def step(i):
            grad, sent = gate(kinds[kind][i].grad, kinds[kind][i].grad_sent)
            if kind == FAR:
                grad, sent = jnp.where(inner, grad, sent), jnp.where(inner, sent, grad)
            grads = stack(grad, sent)
            kinds[kind][i].grads = grads
            kinds[kind][i].grads_other = feat(grads, COLUMN)
            done(grads)

        return step

    def terms(kind):
        def step(i):
            upper, lower = gate(kinds[kind][i].grads, kinds[kind][i].grads_other)
            give, keep = code_terms(core_at, upper, lower, decoder)
            kinds[kind][i].grads, kinds[kind][i].grads_other = upper, lower
            kinds[kind][i].terms = keep
            kinds[kind][i].given = other_core(give)
            done(keep, give)

        return step

    def out1(kind):
        def step(i):
            total = add(*gate(kinds[kind][i].terms, kinds[kind][i].given))
            n = counts[i]
            kinds[kind][i].heres[0], kinds[kind][i].heres[1] = total[:n], total[n : 2 * n]
            kinds[kind][i].waits[0] = total[2 * n : 3 * n]
            kinds[kind][i].theres[1] = feat(total[3 * n :], COLUMN)
            done(total)

        return step

    def out1b(kind):
        def step(i):
            give = gate(kinds[kind][i].waits[0])
            kinds[kind][i].theres[0] = feat(give, COLUMN)
            done(give)

        return step

    def out2(kind, slot):
        def step(i):
            here, there = gate(kinds[kind][i].heres[slot], kinds[kind][i].theres[slot])
            name = named(i, slot + 2 * kind)
            out = jnp.stack(
                [
                    jnp.where(
                        name[:, k : k + 1] == block,
                        here,
                        jnp.where(name[:, k : k + 1] == sibling, there, 0),
                    )
                    for k in range(per_token)
                ]
            )
            kinds[kind][i].ys[slot] = out
            if kind == FAR:
                sent = feat(out, INWARD)
                if slot:
                    parts[i].out_sent = sent
                else:
                    parts[i].in_sent = sent
            done(out)

        return step

    def out3(i):
        y_out = add(*gate(kinds[FAR][i].ys[1], parts[i].out_sent))
        parts[i].out_sent = feat(y_out, MIDDLE)
        done(y_out)

    def out3b(i):
        y_in = add(*gate(kinds[FAR][i].ys[0], parts[i].in_sent))
        parts[i].in_sent = feat(y_in, MIDDLE)
        done(y_in)

    def out4(i):
        y_near = add(*gate(kinds[NEAR][i].ys[1], parts[i].out_sent))
        kinds[NEAR][i].sent = feat(y_near, NEIGHBOUR)
        done(y_near)

    def out5(i):
        own = add(*gate(kinds[NEAR][i].ys[0], kinds[NEAR][i].sent, parts[i].in_sent))
        parts[i].sum = own
        parts[i].sum_other = other_core(own)
        done(own)

    def out6(i):
        own, other = gate(parts[i].sum, parts[i].sum_other)
        first = core == 0
        whole = jnp.concatenate(
            [jnp.where(first, own, other), jnp.where(first, other, own)], axis=2
        )
        parts[i].code_grad = jnp.swapaxes(whole, 0, 1)
        done(parts[i].code_grad)

    def weights(i):
        base = None
        rows, grads = [], []
        for part in range(2):
            for kind in (NEAR, FAR):
                rows.append((kinds[kind][part].rows_other if i else kinds[kind][part].rows))
                grads += [kinds[kind][part].grads, kinds[kind][part].grads_other]
        rows[0] = gate(rows[0])
        if i:
            base = parts[0].weight_grad
        parts[i].weight_grad = weight_half(1 - core_at if i else core_at, rows, grads, base)
        done(parts[i].weight_grad)

    def recon1(i):
        far = gate(kinds[FAR][i].rebuilt)
        kinds[FAR][i].done = feat(far, MIRROR)
        done(far)

    def recon2(i):
        own = stack(kinds[NEAR][0].rebuilt, kinds[NEAR][1].rebuilt)
        far = gate(stack(kinds[FAR][0].done, kinds[FAR][1].done))
        first = target == 0
        parts[0].recon = jnp.stack([jnp.where(first, own, far), jnp.where(first, far, own)], axis=1)
        done(parts[0].recon)

    sums_near, sums_far = sums(NEAR), sums(FAR)
    err1_near, err1_far = err1(NEAR), err1(FAR)
    err2_near, err2_far = err2(NEAR), err2(FAR)
    err3_near, err3_far = err3(NEAR), err3(FAR)
    terms_near, terms_far = terms(NEAR), terms(FAR)
    out1_near, out1_far = out1(NEAR), out1(FAR)
    out1b_near, out1b_far = out1b(NEAR), out1b(FAR)
    out2_mine, out2_next = out2(NEAR, 0), out2(NEAR, 1)
    out2_in, out2_out = out2(FAR, 0), out2(FAR, 1)
    order = (
        (prep, 0), (prep, 1), (ids, 0), (in1, 0), (in1x, 0), (in2, 0), (in3, 0), (sums_near, 0),
        (in4, 0), (in5, 0), (in1, 1), (in1x, 1), (sums_far, 0), (in2, 1), (aims, 0), (in3, 1),
        (err1_far, 0), (sums_near, 1), (in4, 1), (err1_near, 0), (err1_near, 1), (err2_far, 0),
        (aims, 1), (in5, 1), (err3_far, 0), (err2_near, 0), (err2_near, 1), (err3_near, 0),
        (sums_far, 1), (terms_far, 0), (err3_near, 1), (err1_far, 1), (out1_far, 0),
        (err2_far, 1), (recon1, 0), (err3_far, 1), (out1b_far, 0), (out2_out, 0), (terms_far, 1),
        (out2_in, 0), (out3, 0), (recon1, 1), (out1_far, 1), (terms_near, 0), (out2_out, 1),
        (out1_near, 0), (out3b, 0), (out1b_far, 1), (terms_near, 1), (out2_next, 0), (out4, 0),
        (out2_in, 1), (out3, 1), (out1_near, 1), (out1b_near, 0), (out1b_near, 1), (weights, 0),
        (out2_mine, 0), (out5, 0), (out3b, 1), (out2_next, 1), (out4, 1), (weights, 1),
        (out6, 0), (recon2, 0), (out2_mine, 1), (out5, 1), (out6, 1),
    )
    for step, i in order:
        step(i)
    code_grad = stack(parts[0].code_grad, parts[1].code_grad)
    return parts[0].recon, code_grad, parts[1].weight_grad


def solution(mesh):
    owners = mesh.shape["feat"]
    plan = dense if owners // PAIRS == 4 and mesh.shape["pair"] == 2 else slotted
    return jax.shard_map(
        plan,
        mesh=mesh,
        in_specs=(
            P(("groups", "feat"), None, None),
            P(("groups", "feat"), None),
            P("feat", "pair"),
            P(("groups", "feat"), None, "pair"),
        ),
        out_specs=(
            P(("groups", "feat"), None, "pair"),
            P(("groups", "feat"), None, None),
            P(("groups", "feat"), "pair"),
        ),
        check_vma=False,
    )
```

```python
import jax
import jax.numpy as jnp
from jax import lax
from jax.experimental import pallas as pl
from jax.experimental.pallas import tpu as pltpu
from jax.sharding import PartitionSpec as P

PAIRS = 2
SPLIT = (1, 1)
STRIP = 1024
DEEP = 2048
VMEM_LIMIT = 48 * 1024 * 1024


error_scale = 0.125


def slotted(codes, block_ids, decoder, targets):
    tok_rows, per_token, block_width = codes.shape
    half_width = decoder.shape[1]
    owners = lax.axis_size("feat")
    blocks = owners // PAIRS
    capacity = 2 * tok_rows * per_token // blocks
    flat_ids = block_ids.reshape(-1)
    matches = (flat_ids[:, None] == jnp.arange(blocks, dtype=jnp.int32)[None, :]).astype(jnp.int32)
    ranking = jnp.sum((jnp.cumsum(matches, axis=0) - 1) * matches, axis=1)
    slot_lists = [(target * blocks + flat_ids) * capacity + ranking for target in range(PAIRS)]
    values = codes.reshape(-1, block_width)
    outgoing = jnp.zeros((owners * capacity, values.shape[1]), jnp.bfloat16)
    for slot_index in slot_lists:
        outgoing = outgoing.at[slot_index].set(values)
    outgoing = outgoing.reshape(owners, capacity, values.shape[1])
    arrived = lax.all_to_all(outgoing, "feat", split_axis=0, concat_axis=0, tiled=True)
    partial_rows = jnp.einsum("snb,bd->snd", arrived, decoder, preferred_element_type=jnp.float32)
    sent_back = lax.all_to_all(
        partial_rows.astype(jnp.bfloat16), "feat", split_axis=0, concat_axis=0, tiled=True
    )
    returned_flat = sent_back.reshape(owners * capacity, half_width)
    rebuilt = jnp.stack(
        [
            jnp.sum(
                returned_flat[slot_index]
                .astype(jnp.float32)
                .reshape(tok_rows, per_token, half_width),
                axis=1,
            )
            for slot_index in slot_lists
        ],
        axis=1,
    )
    error_grad = ((rebuilt - targets.astype(jnp.float32)) * error_scale).astype(jnp.bfloat16)
    grad_out = jnp.zeros((owners * capacity, half_width), jnp.bfloat16)
    for target in range(PAIRS):
        grad_out = grad_out.at[slot_lists[target]].set(
            jnp.repeat(error_grad[:, target], per_token, axis=0)
        )
    grad_out = grad_out.reshape(owners, capacity, half_width)
    arrived_grad = lax.all_to_all(grad_out, "feat", split_axis=0, concat_axis=0, tiled=True)
    summed = jnp.einsum("snd,bd->snb", arrived_grad, decoder, preferred_element_type=jnp.float32)
    summed = lax.psum(summed, "pair")
    sent_back = lax.all_to_all(
        summed.astype(jnp.bfloat16), "feat", split_axis=0, concat_axis=0, tiled=True
    )
    weight_grad = lax.dot_general(
        arrived.reshape(-1, block_width),
        arrived_grad.reshape(-1, half_width),
        (((0,), (0,)), ((), ())),
        preferred_element_type=jnp.float32,
    ).astype(jnp.bfloat16)
    code_flat = sent_back.reshape(owners * capacity, sent_back.shape[2])
    code_total = code_flat[slot_lists[0]].astype(jnp.float32)
    for slot_index in slot_lists[1:]:
        code_total = code_total + code_flat[slot_index].astype(jnp.float32)
    code_grad = code_total.astype(jnp.bfloat16).reshape(tok_rows, per_token, sent_back.shape[2])
    return (rebuilt.astype(jnp.bfloat16), code_grad, weight_grad)


def add(*terms):
    return sum(term.astype(jnp.float32) for term in terms).astype(jnp.bfloat16)


def call(kernel, core, operands, specs, grid, outs, out_specs, scratch, flops, moved, alias={}):
    return pl.pallas_call(
        kernel,
        grid_spec=pltpu.PrefetchScalarGridSpec(
            num_scalar_prefetch=1,
            grid=(grid,),
            in_specs=specs,
            out_specs=out_specs,
            scratch_shapes=scratch,
        ),
        out_shape=outs,
        input_output_aliases=alias,
        compiler_params=pltpu.CompilerParams(
            vmem_limit_bytes=VMEM_LIMIT, dimension_semantics=("arbitrary",)
        ),
        cost_estimate=pl.CostEstimate(flops=flops, bytes_accessed=moved, transcendentals=0),
    )(core, *operands)


def rebuild(core, own, other, decoder):
    rows, half = own.shape
    depth = decoder.shape[1]
    strips = half // min(DEEP, half)
    kept = rows // 2

    def kernel(core_ref, own_ref, other_ref, decoder_ref, *rest):
        upper_ref, lower_ref, total = rest[-3:]
        step = pl.program_id(0)

        @pl.when(step == 0)
        def _():
            total[...] = jnp.zeros_like(total)

        @pl.when(step < strips)
        def _():
            total[...] += jnp.dot(
                own_ref[...], decoder_ref[...], preferred_element_type=jnp.float32
            )

        @pl.when(step >= strips)
        def _():
            total[...] += jnp.dot(
                other_ref[...], decoder_ref[...], preferred_element_type=jnp.float32
            )

        @pl.when(step == 2 * strips - 1)
        def _():
            upper_ref[...] = total[:kept].astype(jnp.bfloat16)
            lower_ref[...] = total[kept:].astype(jnp.bfloat16)

    def strip(step, core_ref):
        side = jnp.where(step < strips, core_ref[0], 1 - core_ref[0])
        return side * strips + lax.rem(step, strips), 0

    out = jax.ShapeDtypeStruct((kept, depth), jnp.bfloat16)
    return call(
        kernel,
        core,
        [own, other, decoder],
        [
            pl.BlockSpec((rows, DEEP), lambda i, c: (0, jnp.minimum(i, strips - 1))),
            pl.BlockSpec((rows, DEEP), lambda i, c: (0, jnp.maximum(i - strips, 0))),
            pl.BlockSpec((DEEP, depth), strip),
        ],
        2 * strips,
        [out, out],
        [pl.BlockSpec((kept, depth), lambda i, c: (0, 0))] * 2,
        [pltpu.VMEM((rows, depth), jnp.float32)],
        4 * rows * half * depth,
        4 * half * depth,
    )


def code_terms(core, upper, lower, decoder):
    kept, depth = upper.shape
    half = decoder.shape[0] // 2
    strips = half // min(STRIP, half)
    rows = 2 * kept

    def kernel(core_ref, upper_ref, lower_ref, decoder_ref, give_ref, keep_ref, grads):
        step = pl.program_id(0)

        @pl.when(step == 0)
        def _():
            grads[:kept, :] = upper_ref[...]
            grads[kept:, :] = lower_ref[...]

        product = lax.dot_general(
            grads[...],
            decoder_ref[...],
            (((1,), (1,)), ((), ())),
            preferred_element_type=jnp.float32,
        ).astype(jnp.bfloat16)

        @pl.when(step < strips)
        def _():
            give_ref[...] = product

        @pl.when(step >= strips)
        def _():
            keep_ref[...] = product

    def strip(step, core_ref):
        side = jnp.where(step < strips, 1 - core_ref[0], core_ref[0])
        return side * strips + lax.rem(step, strips), 0

    out = jax.ShapeDtypeStruct((rows, half), jnp.bfloat16)
    return call(
        kernel,
        core,
        [upper, lower, decoder],
        [pl.BlockSpec((kept, depth), lambda i, c: (0, 0))] * 2
        + [pl.BlockSpec((STRIP, depth), strip)],
        2 * strips,
        [out, out],
        [
            pl.BlockSpec((rows, STRIP), lambda i, c: (0, jnp.minimum(i, strips - 1))),
            pl.BlockSpec((rows, STRIP), lambda i, c: (0, jnp.maximum(i - strips, 0))),
        ],
        [pltpu.VMEM((rows, depth), jnp.bfloat16)],
        4 * rows * half * depth,
        4 * half * depth,
    )


def weight_half(side, rows, grads, base=None):
    half = rows[0].shape[1]
    depth = grads[0].shape[1]
    strips = half // min(STRIP, half)
    sizes = [piece.shape[0] for piece in grads]
    total = sum(sizes)
    pieces = len(rows)

    def kernel(side_ref, *refs):
        row_refs, grad_refs = refs[:pieces], refs[pieces : pieces + len(grads)]
        out_ref, stacked = refs[-2:]

        @pl.when(pl.program_id(0) == 0)
        def _():
            at = 0
            for size, ref in zip(sizes, grad_refs):
                stacked[at : at + size, :] = ref[...]
                at += size

        left = jnp.concatenate([ref[...] for ref in row_refs], axis=0)
        out_ref[...] = lax.dot_general(
            left, stacked[...], (((0,), (0,)), ((), ())), preferred_element_type=jnp.float32
        ).astype(jnp.bfloat16)

    operands = rows + grads
    specs = [pl.BlockSpec((piece.shape[0], STRIP), lambda i, c: (0, i)) for piece in rows]
    specs += [pl.BlockSpec(piece.shape, lambda i, c: (0, 0)) for piece in grads]
    alias = {}
    if base is not None:
        alias = {1 + len(operands): 0}
        operands = operands + [base]
        specs = specs + [pl.BlockSpec(memory_space=pl.ANY)]
    return call(
        kernel,
        side,
        operands,
        specs,
        strips,
        jax.ShapeDtypeStruct((2 * half, depth), jnp.bfloat16),
        pl.BlockSpec((STRIP, depth), lambda i, c: (c[0] * strips + i, 0)),
        [pltpu.VMEM((total, depth), jnp.bfloat16)],
        2 * total * half * depth,
        2 * half * (depth + total),
        alias,
    )


NEAR, FAR = 0, 1


class Bag:
    def __init__(self):
        self.heres, self.theres, self.waits, self.ys = ([None, None] for _ in range(4))


def dense(codes, block_ids, decoder, targets):
    tok_rows, per_token, width = codes.shape
    half = width // 2
    me = lax.axis_index("feat")
    core = lax.axis_index("pair")
    core_at = core.astype(jnp.int32).reshape(1)
    layer = me // 2
    target = layer // 2
    inner = (layer == 1) | (layer == 2)
    block = me % 4
    sibling = block ^ 1
    unit = tok_rows // sum(SPLIT)
    starts = (0, SPLIT[0] * unit)
    counts = (SPLIT[0] * unit, tok_rows - SPLIT[0] * unit)

    def over_layers(pairs):
        return [(a * 2 + x, b * 2 + x) for a, b in pairs for x in range(2)]

    def feat(value, perm):
        return lax.ppermute(value, "feat", perm)

    NEIGHBOUR = over_layers([(0, 1), (1, 0), (2, 3), (3, 2)])
    MIDDLE = over_layers([(1, 2), (2, 1)])
    OUTWARD = over_layers([(1, 0), (2, 3)])
    INWARD = over_layers([(0, 1), (3, 2)])
    MIRROR = over_layers([(0, 3), (3, 0), (1, 2), (2, 1)])
    ACROSS = over_layers([(0, 2), (2, 0), (1, 3), (3, 1)])
    COLUMN = [(i, i ^ 1) for i in range(8)]

    def other_core(value):
        return lax.ppermute(value, "pair", [(0, 1), (1, 0)])

    def pick(value, ids, wanted):
        hits = (ids == wanted)[:, :, None]
        return jnp.where(hits[:, 0], value[0], jnp.where(hits[:, 1], value[1], 0))

    def stack(*values):
        return jnp.concatenate(values, axis=0)

    def part_of(value, i):
        return value[starts[i] : starts[i] + counts[i]]

    def error(rebuilt, wanted):
        gap = rebuilt.astype(jnp.float32) - wanted.astype(jnp.float32)
        return (gap * error_scale).astype(jnp.bfloat16)

    parts = (Bag(), Bag())
    kinds = tuple((Bag(), Bag()) for kind in (NEAR, FAR))
    token = []

    def gate(*values):
        out = lax.optimization_barrier((*values, *token))[: len(values)]
        return out[0] if len(values) == 1 else out

    def done(*values):
        token[:] = values

    def prep(i):
        source = codes if i == 0 else gate(codes)
        own = lax.dynamic_slice(source, (starts[i], 0, core * half), (counts[i], per_token, half))
        own = jnp.swapaxes(own, 0, 1)
        parts[i].own = own
        if i == 0:
            parts[i].near = feat(own, NEIGHBOUR)
            parts[i].mid = feat(own, MIDDLE)
        done(own)

    def ids(i):
        parts[i].near, parts[i].mid, mine = gate(parts[i].near, parts[i].mid, block_ids)
        near, mirror, across = feat(mine, NEIGHBOUR), feat(mine, MIRROR), feat(mine, ACROSS)
        parts[0].slots = [
            block_ids,
            near,
            jnp.where(inner, mirror, across),
            jnp.where(inner, across, mirror),
        ]
        done(mine)

    def aims(i):
        wanted = part_of(gate(targets), i)
        kinds[NEAR][i].aim = lax.dynamic_index_in_dim(wanted, target, 1, keepdims=False)
        far = lax.dynamic_index_in_dim(wanted, 1 - target, 1, keepdims=False)
        kinds[FAR][i].aim = feat(far, MIRROR)
        done(far, kinds[NEAR][i].aim)

    def named(i, slot):
        return part_of(parts[0].slots[slot], i)

    def in1(i):
        near, mid = gate(parts[i].near, parts[i].mid)
        parts[i].in_end = feat(mid, OUTWARD)
        parts[i].out_mid = feat(near, MIDDLE)
        parts[i].near, parts[i].mid = near, mid
        done(near, mid)

    def in1x(i):
        own, near = gate(parts[i].own, parts[i].near)
        a, b = named(i, 0), named(i, 1)
        crossing = stack(pick(own, a, sibling), pick(near, b, sibling))
        kinds[NEAR][i].crossed = feat(crossing, COLUMN)
        kinds[NEAR][i].kept = stack(pick(own, a, block), pick(near, b, block))
        done(crossing, kinds[NEAR][i].kept)

    def in2(i):
        in_end, out_mid, mid = gate(parts[i].in_end, parts[i].out_mid, parts[i].mid)
        parts[i].out_end = feat(out_mid, OUTWARD)
        parts[i].out_mid = out_mid
        if i == 0:
            parts[1].mid = feat(gate(parts[1].own), MIDDLE)
        far_in = jnp.where(inner, mid, in_end)
        crossing = pick(far_in, named(i, 2), sibling)
        parts[i].in_crossed = feat(crossing, COLUMN)
        parts[i].in_kept = pick(far_in, named(i, 2), block)
        done(crossing, parts[i].in_kept)

    def in3(i):
        kept, crossed = gate(kinds[NEAR][i].kept, kinds[NEAR][i].crossed)
        rows = stack(kept, crossed)
        kinds[NEAR][i].rows = rows
        kinds[NEAR][i].rows_other = other_core(rows)
        done(rows)

    def in4(i):
        out_end, out_mid = gate(parts[i].out_end, parts[i].out_mid)
        if i == 0:
            parts[1].near = feat(gate(parts[1].own), NEIGHBOUR)
        far_out = jnp.where(inner, out_mid, out_end)
        crossing = pick(far_out, named(i, 3), sibling)
        parts[i].out_crossed = feat(crossing, COLUMN)
        parts[i].out_kept = pick(far_out, named(i, 3), block)
        done(crossing, parts[i].out_kept)

    def in5(i):
        rows = stack(*gate(parts[i].in_kept, parts[i].out_kept, parts[i].in_crossed, parts[i].out_crossed))
        kinds[FAR][i].rows = rows
        kinds[FAR][i].rows_other = other_core(rows)
        done(rows)

    def sums(kind):
        def step(i):
            own, other = gate(kinds[kind][i].rows, kinds[kind][i].rows_other)
            upper, lower = rebuild(core_at, own, other, decoder)
            kinds[kind][i].rows, kinds[kind][i].rows_other = own, other
            kinds[kind][i].upper = upper
            kinds[kind][i].lower = feat(lower, COLUMN)
            done(upper, lower)

        return step

    def err1(kind):
        def step(i):
            total = add(*gate(kinds[kind][i].upper, kinds[kind][i].lower))
            first, second = total[: counts[i]], total[counts[i] :]
            keep, send = first, second
            if kind == FAR:
                keep, send = jnp.where(inner, first, second), jnp.where(inner, second, first)
            kinds[kind][i].keep = keep
            kinds[kind][i].sent = feat(send, NEIGHBOUR)
            done(keep, send)

        return step

    def err2(kind):
        def step(i):
            rebuilt = add(*gate(kinds[kind][i].keep, kinds[kind][i].sent))
            grad = error(rebuilt, gate(kinds[kind][i].aim))
            kinds[kind][i].rebuilt = rebuilt
            kinds[kind][i].grad = grad
            kinds[kind][i].grad_sent = feat(grad, NEIGHBOUR)
            done(grad)

        return step

    def err3(kind):
        def step(i):
            grad, sent = gate(kinds[kind][i].grad, kinds[kind][i].grad_sent)
            if kind == FAR:
                grad, sent = jnp.where(inner, grad, sent), jnp.where(inner, sent, grad)
            grads = stack(grad, sent)
            kinds[kind][i].grads = grads
            kinds[kind][i].grads_other = feat(grads, COLUMN)
            done(grads)

        return step

    def terms(kind):
        def step(i):
            upper, lower = gate(kinds[kind][i].grads, kinds[kind][i].grads_other)
            give, keep = code_terms(core_at, upper, lower, decoder)
            kinds[kind][i].grads, kinds[kind][i].grads_other = upper, lower
            kinds[kind][i].terms = keep
            kinds[kind][i].given = other_core(give)
            done(keep, give)

        return step

    def out1(kind):
        def step(i):
            total = add(*gate(kinds[kind][i].terms, kinds[kind][i].given))
            n = counts[i]
            kinds[kind][i].heres[0], kinds[kind][i].heres[1] = total[:n], total[n : 2 * n]
            kinds[kind][i].waits[0] = total[2 * n : 3 * n]
            kinds[kind][i].theres[1] = feat(total[3 * n :], COLUMN)
            done(total)

        return step

    def out1b(kind):
        def step(i):
            give = gate(kinds[kind][i].waits[0])
            kinds[kind][i].theres[0] = feat(give, COLUMN)
            done(give)

        return step

    def out2(kind, slot):
        def step(i):
            here, there = gate(kinds[kind][i].heres[slot], kinds[kind][i].theres[slot])
            name = named(i, slot + 2 * kind)
            out = jnp.stack(
                [
                    jnp.where(
                        name[:, k : k + 1] == block,
                        here,
                        jnp.where(name[:, k : k + 1] == sibling, there, 0),
                    )
                    for k in range(per_token)
                ]
            )
            kinds[kind][i].ys[slot] = out
            if kind == FAR:
                sent = feat(out, INWARD)
                if slot:
                    parts[i].out_sent = sent
                else:
                    parts[i].in_sent = sent
            done(out)

        return step

    def out3(i):
        y_out = add(*gate(kinds[FAR][i].ys[1], parts[i].out_sent))
        parts[i].out_sent = feat(y_out, MIDDLE)
        done(y_out)

    def out3b(i):
        y_in = add(*gate(kinds[FAR][i].ys[0], parts[i].in_sent))
        parts[i].in_sent = feat(y_in, MIDDLE)
        done(y_in)

    def out4(i):
        y_near = add(*gate(kinds[NEAR][i].ys[1], parts[i].out_sent))
        kinds[NEAR][i].sent = feat(y_near, NEIGHBOUR)
        done(y_near)

    def out5(i):
        own = add(*gate(kinds[NEAR][i].ys[0], kinds[NEAR][i].sent, parts[i].in_sent))
        parts[i].sum = own
        parts[i].sum_other = other_core(own)
        done(own)

    def out6(i):
        own, other = gate(parts[i].sum, parts[i].sum_other)
        first = core == 0
        whole = jnp.concatenate(
            [jnp.where(first, own, other), jnp.where(first, other, own)], axis=2
        )
        parts[i].code_grad = jnp.swapaxes(whole, 0, 1)
        done(parts[i].code_grad)

    def weights(i):
        base = None
        rows, grads = [], []
        for part in range(2):
            for kind in (NEAR, FAR):
                rows.append((kinds[kind][part].rows_other if i else kinds[kind][part].rows))
                grads += [kinds[kind][part].grads, kinds[kind][part].grads_other]
        rows[0] = gate(rows[0])
        if i:
            base = parts[0].weight_grad
        parts[i].weight_grad = weight_half(1 - core_at if i else core_at, rows, grads, base)
        done(parts[i].weight_grad)

    def recon1(i):
        far = gate(kinds[FAR][i].rebuilt)
        kinds[FAR][i].done = feat(far, MIRROR)
        done(far)

    def recon2(i):
        own = stack(kinds[NEAR][0].rebuilt, kinds[NEAR][1].rebuilt)
        far = gate(stack(kinds[FAR][0].done, kinds[FAR][1].done))
        first = target == 0
        parts[0].recon = jnp.stack([jnp.where(first, own, far), jnp.where(first, far, own)], axis=1)
        done(parts[0].recon)

    sums_near, sums_far = sums(NEAR), sums(FAR)
    err1_near, err1_far = err1(NEAR), err1(FAR)
    err2_near, err2_far = err2(NEAR), err2(FAR)
    err3_near, err3_far = err3(NEAR), err3(FAR)
    terms_near, terms_far = terms(NEAR), terms(FAR)
    out1_near, out1_far = out1(NEAR), out1(FAR)
    out1b_near, out1b_far = out1b(NEAR), out1b(FAR)
    out2_mine, out2_next = out2(NEAR, 0), out2(NEAR, 1)
    out2_in, out2_out = out2(FAR, 0), out2(FAR, 1)
    order = (
        (prep, 0), (prep, 1), (ids, 0), (in1, 0), (in1x, 0), (in2, 0), (in3, 0), (sums_near, 0),
        (in4, 0), (in5, 0), (in1, 1), (in1x, 1), (sums_far, 0), (in2, 1), (aims, 0), (in3, 1),
        (err1_far, 0), (sums_near, 1), (in4, 1), (err1_near, 0), (err1_near, 1), (err2_far, 0),
        (aims, 1), (in5, 1), (err3_far, 0), (err2_near, 0), (err2_near, 1), (err3_near, 0),
        (sums_far, 1), (terms_far, 0), (err3_near, 1), (err1_far, 1), (out1_far, 0),
        (err2_far, 1), (recon1, 0), (err3_far, 1), (out1b_far, 0), (out2_out, 0), (terms_far, 1),
        (out2_in, 0), (out3, 0), (recon1, 1), (out1_far, 1), (terms_near, 0), (out2_out, 1),
        (out1_near, 0), (out3b, 0), (out1b_far, 1), (terms_near, 1), (out2_next, 0), (out4, 0),
        (out2_in, 1), (out3, 1), (out1_near, 1), (out1b_near, 0), (out1b_near, 1), (weights, 0),
        (out2_mine, 0), (out5, 0), (out3b, 1), (out2_next, 1), (out4, 1), (weights, 1),
        (out6, 0), (recon2, 0), (out2_mine, 1), (out5, 1), (out6, 1),
    )
    for step, i in order:
        step(i)
    code_grad = stack(parts[0].code_grad, parts[1].code_grad)
    return parts[0].recon, code_grad, parts[1].weight_grad


def solution(mesh):
    owners = mesh.shape["feat"]
    plan = dense if owners // PAIRS == 4 and mesh.shape["pair"] == 2 else slotted
    return jax.shard_map(
        plan,
        mesh=mesh,
        in_specs=(
            P(("groups", "feat"), None, None),
            P(("groups", "feat"), None),
            P("feat", "pair"),
            P(("groups", "feat"), None, "pair"),
        ),
        out_specs=(
            P(("groups", "feat"), None, "pair"),
            P(("groups", "feat"), None, None),
            P(("groups", "feat"), "pair"),
        ),
        check_vma=False,
    )
```

```python
import jax
import jax.numpy as jnp
from jax import lax
from jax.experimental import pallas as pl
from jax.experimental.pallas import tpu as pltpu
from jax.sharding import PartitionSpec as P

PAIRS = 2
SPLIT = (1, 1)
STRIP = 1024
DEEP = 2048
VMEM_LIMIT = 48 * 1024 * 1024


error_scale = 0.125


def slotted(codes, block_ids, decoder, targets):
    tok_rows, per_token, block_width = codes.shape
    half_width = decoder.shape[1]
    owners = lax.axis_size("feat")
    blocks = owners // PAIRS
    capacity = 2 * tok_rows * per_token // blocks
    flat_ids = block_ids.reshape(-1)
    matches = (flat_ids[:, None] == jnp.arange(blocks, dtype=jnp.int32)[None, :]).astype(jnp.int32)
    ranking = jnp.sum((jnp.cumsum(matches, axis=0) - 1) * matches, axis=1)
    slot_lists = [(target * blocks + flat_ids) * capacity + ranking for target in range(PAIRS)]
    values = codes.reshape(-1, block_width)
    outgoing = jnp.zeros((owners * capacity, values.shape[1]), jnp.bfloat16)
    for slot_index in slot_lists:
        outgoing = outgoing.at[slot_index].set(values)
    outgoing = outgoing.reshape(owners, capacity, values.shape[1])
    arrived = lax.all_to_all(outgoing, "feat", split_axis=0, concat_axis=0, tiled=True)
    partial_rows = jnp.einsum("snb,bd->snd", arrived, decoder, preferred_element_type=jnp.float32)
    sent_back = lax.all_to_all(
        partial_rows.astype(jnp.bfloat16), "feat", split_axis=0, concat_axis=0, tiled=True
    )
    returned_flat = sent_back.reshape(owners * capacity, half_width)
    rebuilt = jnp.stack(
        [
            jnp.sum(
                returned_flat[slot_index]
                .astype(jnp.float32)
                .reshape(tok_rows, per_token, half_width),
                axis=1,
            )
            for slot_index in slot_lists
        ],
        axis=1,
    )
    error_grad = ((rebuilt - targets.astype(jnp.float32)) * error_scale).astype(jnp.bfloat16)
    grad_out = jnp.zeros((owners * capacity, half_width), jnp.bfloat16)
    for target in range(PAIRS):
        grad_out = grad_out.at[slot_lists[target]].set(
            jnp.repeat(error_grad[:, target], per_token, axis=0)
        )
    grad_out = grad_out.reshape(owners, capacity, half_width)
    arrived_grad = lax.all_to_all(grad_out, "feat", split_axis=0, concat_axis=0, tiled=True)
    summed = jnp.einsum("snd,bd->snb", arrived_grad, decoder, preferred_element_type=jnp.float32)
    summed = lax.psum(summed, "pair")
    sent_back = lax.all_to_all(
        summed.astype(jnp.bfloat16), "feat", split_axis=0, concat_axis=0, tiled=True
    )
    weight_grad = lax.dot_general(
        arrived.reshape(-1, block_width),
        arrived_grad.reshape(-1, half_width),
        (((0,), (0,)), ((), ())),
        preferred_element_type=jnp.float32,
    ).astype(jnp.bfloat16)
    code_flat = sent_back.reshape(owners * capacity, sent_back.shape[2])
    code_total = code_flat[slot_lists[0]].astype(jnp.float32)
    for slot_index in slot_lists[1:]:
        code_total = code_total + code_flat[slot_index].astype(jnp.float32)
    code_grad = code_total.astype(jnp.bfloat16).reshape(tok_rows, per_token, sent_back.shape[2])
    return (rebuilt.astype(jnp.bfloat16), code_grad, weight_grad)


def add(*terms):
    return sum(term.astype(jnp.float32) for term in terms).astype(jnp.bfloat16)


def call(kernel, core, operands, specs, grid, outs, out_specs, scratch, flops, moved, alias={}):
    return pl.pallas_call(
        kernel,
        grid_spec=pltpu.PrefetchScalarGridSpec(
            num_scalar_prefetch=1,
            grid=(grid,),
            in_specs=specs,
            out_specs=out_specs,
            scratch_shapes=scratch,
        ),
        out_shape=outs,
        input_output_aliases=alias,
        compiler_params=pltpu.CompilerParams(
            vmem_limit_bytes=VMEM_LIMIT, dimension_semantics=("arbitrary",)
        ),
        cost_estimate=pl.CostEstimate(flops=flops, bytes_accessed=moved, transcendentals=0),
    )(core, *operands)


def rebuild(core, own, other, decoder):
    rows, half = own.shape
    depth = decoder.shape[1]
    strips = half // min(DEEP, half)
    kept = rows // 2

    def kernel(core_ref, own_ref, other_ref, decoder_ref, *rest):
        upper_ref, lower_ref, total = rest[-3:]
        step = pl.program_id(0)

        @pl.when(step == 0)
        def _():
            total[...] = jnp.zeros_like(total)

        @pl.when(step < strips)
        def _():
            total[...] += jnp.dot(
                own_ref[...], decoder_ref[...], preferred_element_type=jnp.float32
            )

        @pl.when(step >= strips)
        def _():
            total[...] += jnp.dot(
                other_ref[...], decoder_ref[...], preferred_element_type=jnp.float32
            )

        @pl.when(step == 2 * strips - 1)
        def _():
            upper_ref[...] = total[:kept].astype(jnp.bfloat16)
            lower_ref[...] = total[kept:].astype(jnp.bfloat16)

    def strip(step, core_ref):
        side = jnp.where(step < strips, core_ref[0], 1 - core_ref[0])
        return side * strips + lax.rem(step, strips), 0

    out = jax.ShapeDtypeStruct((kept, depth), jnp.bfloat16)
    return call(
        kernel,
        core,
        [own, other, decoder],
        [
            pl.BlockSpec((rows, DEEP), lambda i, c: (0, jnp.minimum(i, strips - 1))),
            pl.BlockSpec((rows, DEEP), lambda i, c: (0, jnp.maximum(i - strips, 0))),
            pl.BlockSpec((DEEP, depth), strip),
        ],
        2 * strips,
        [out, out],
        [pl.BlockSpec((kept, depth), lambda i, c: (0, 0))] * 2,
        [pltpu.VMEM((rows, depth), jnp.float32)],
        4 * rows * half * depth,
        4 * half * depth,
    )


def code_terms(core, upper, lower, decoder):
    kept, depth = upper.shape
    half = decoder.shape[0] // 2
    strips = half // min(DEEP, half)
    rows = 2 * kept

    def kernel(core_ref, upper_ref, lower_ref, decoder_ref, give_ref, keep_ref, grads):
        step = pl.program_id(0)

        @pl.when(step == 0)
        def _():
            grads[:kept, :] = upper_ref[...]
            grads[kept:, :] = lower_ref[...]

        product = lax.dot_general(
            grads[...],
            decoder_ref[...],
            (((1,), (1,)), ((), ())),
            preferred_element_type=jnp.float32,
        ).astype(jnp.bfloat16)

        @pl.when(step < strips)
        def _():
            give_ref[...] = product

        @pl.when(step >= strips)
        def _():
            keep_ref[...] = product

    def strip(step, core_ref):
        side = jnp.where(step < strips, 1 - core_ref[0], core_ref[0])
        return side * strips + lax.rem(step, strips), 0

    out = jax.ShapeDtypeStruct((rows, half), jnp.bfloat16)
    return call(
        kernel,
        core,
        [upper, lower, decoder],
        [pl.BlockSpec((kept, depth), lambda i, c: (0, 0))] * 2
        + [pl.BlockSpec((DEEP, depth), strip)],
        2 * strips,
        [out, out],
        [
            pl.BlockSpec((rows, DEEP), lambda i, c: (0, jnp.minimum(i, strips - 1))),
            pl.BlockSpec((rows, DEEP), lambda i, c: (0, jnp.maximum(i - strips, 0))),
        ],
        [pltpu.VMEM((rows, depth), jnp.bfloat16)],
        4 * rows * half * depth,
        4 * half * depth,
    )


def weight_half(side, rows, grads, base=None):
    half = rows[0].shape[1]
    depth = grads[0].shape[1]
    strips = half // min(STRIP, half)
    sizes = [piece.shape[0] for piece in grads]
    total = sum(sizes)
    pieces = len(rows)

    def kernel(side_ref, *refs):
        row_refs, grad_refs = refs[:pieces], refs[pieces : pieces + len(grads)]
        out_ref, stacked = refs[-2:]

        @pl.when(pl.program_id(0) == 0)
        def _():
            at = 0
            for size, ref in zip(sizes, grad_refs):
                stacked[at : at + size, :] = ref[...]
                at += size

        left = jnp.concatenate([ref[...] for ref in row_refs], axis=0)
        out_ref[...] = lax.dot_general(
            left, stacked[...], (((0,), (0,)), ((), ())), preferred_element_type=jnp.float32
        ).astype(jnp.bfloat16)

    operands = rows + grads
    specs = [pl.BlockSpec((piece.shape[0], STRIP), lambda i, c: (0, i)) for piece in rows]
    specs += [pl.BlockSpec(piece.shape, lambda i, c: (0, 0)) for piece in grads]
    alias = {}
    if base is not None:
        alias = {1 + len(operands): 0}
        operands = operands + [base]
        specs = specs + [pl.BlockSpec(memory_space=pl.ANY)]
    return call(
        kernel,
        side,
        operands,
        specs,
        strips,
        jax.ShapeDtypeStruct((2 * half, depth), jnp.bfloat16),
        pl.BlockSpec((STRIP, depth), lambda i, c: (c[0] * strips + i, 0)),
        [pltpu.VMEM((total, depth), jnp.bfloat16)],
        2 * total * half * depth,
        2 * half * (depth + total),
        alias,
    )


NEAR, FAR = 0, 1


class Bag:
    def __init__(self):
        self.heres, self.theres, self.waits, self.ys = ([None, None] for _ in range(4))


def dense(codes, block_ids, decoder, targets):
    tok_rows, per_token, width = codes.shape
    half = width // 2
    me = lax.axis_index("feat")
    core = lax.axis_index("pair")
    core_at = core.astype(jnp.int32).reshape(1)
    layer = me // 2
    target = layer // 2
    inner = (layer == 1) | (layer == 2)
    block = me % 4
    sibling = block ^ 1
    unit = tok_rows // sum(SPLIT)
    starts = (0, SPLIT[0] * unit)
    counts = (SPLIT[0] * unit, tok_rows - SPLIT[0] * unit)

    def over_layers(pairs):
        return [(a * 2 + x, b * 2 + x) for a, b in pairs for x in range(2)]

    def feat(value, perm):
        return lax.ppermute(value, "feat", perm)

    NEIGHBOUR = over_layers([(0, 1), (1, 0), (2, 3), (3, 2)])
    MIDDLE = over_layers([(1, 2), (2, 1)])
    OUTWARD = over_layers([(1, 0), (2, 3)])
    INWARD = over_layers([(0, 1), (3, 2)])
    MIRROR = over_layers([(0, 3), (3, 0), (1, 2), (2, 1)])
    ACROSS = over_layers([(0, 2), (2, 0), (1, 3), (3, 1)])
    COLUMN = [(i, i ^ 1) for i in range(8)]

    def other_core(value):
        return lax.ppermute(value, "pair", [(0, 1), (1, 0)])

    def pick(value, ids, wanted):
        hits = (ids == wanted)[:, :, None]
        return jnp.where(hits[:, 0], value[0], jnp.where(hits[:, 1], value[1], 0))

    def stack(*values):
        return jnp.concatenate(values, axis=0)

    def part_of(value, i):
        return value[starts[i] : starts[i] + counts[i]]

    def error(rebuilt, wanted):
        gap = rebuilt.astype(jnp.float32) - wanted.astype(jnp.float32)
        return (gap * error_scale).astype(jnp.bfloat16)

    parts = (Bag(), Bag())
    kinds = tuple((Bag(), Bag()) for kind in (NEAR, FAR))
    token = []

    def gate(*values):
        out = lax.optimization_barrier((*values, *token))[: len(values)]
        return out[0] if len(values) == 1 else out

    def done(*values):
        token[:] = values

    def prep(i):
        source = codes if i == 0 else gate(codes)
        own = lax.dynamic_slice(source, (starts[i], 0, core * half), (counts[i], per_token, half))
        own = jnp.swapaxes(own, 0, 1)
        parts[i].own = own
        if i == 0:
            parts[i].near = feat(own, NEIGHBOUR)
            parts[i].mid = feat(own, MIDDLE)
        done(own)

    def ids(i):
        parts[i].near, parts[i].mid, mine = gate(parts[i].near, parts[i].mid, block_ids)
        near, mirror, across = feat(mine, NEIGHBOUR), feat(mine, MIRROR), feat(mine, ACROSS)
        parts[0].slots = [
            block_ids,
            near,
            jnp.where(inner, mirror, across),
            jnp.where(inner, across, mirror),
        ]
        done(mine)

    def aims(i):
        wanted = part_of(gate(targets), i)
        kinds[NEAR][i].aim = lax.dynamic_index_in_dim(wanted, target, 1, keepdims=False)
        far = lax.dynamic_index_in_dim(wanted, 1 - target, 1, keepdims=False)
        kinds[FAR][i].aim = feat(far, MIRROR)
        done(far, kinds[NEAR][i].aim)

    def named(i, slot):
        return part_of(parts[0].slots[slot], i)

    def in1(i):
        near, mid = gate(parts[i].near, parts[i].mid)
        parts[i].in_end = feat(mid, OUTWARD)
        parts[i].out_mid = feat(near, MIDDLE)
        parts[i].near, parts[i].mid = near, mid
        done(near, mid)

    def in1x(i):
        own, near = gate(parts[i].own, parts[i].near)
        a, b = named(i, 0), named(i, 1)
        crossing = stack(pick(own, a, sibling), pick(near, b, sibling))
        kinds[NEAR][i].crossed = feat(crossing, COLUMN)
        kinds[NEAR][i].kept = stack(pick(own, a, block), pick(near, b, block))
        done(crossing, kinds[NEAR][i].kept)

    def in2(i):
        in_end, out_mid, mid = gate(parts[i].in_end, parts[i].out_mid, parts[i].mid)
        parts[i].out_end = feat(out_mid, OUTWARD)
        parts[i].out_mid = out_mid
        if i == 0:
            parts[1].mid = feat(gate(parts[1].own), MIDDLE)
        far_in = jnp.where(inner, mid, in_end)
        crossing = pick(far_in, named(i, 2), sibling)
        parts[i].in_crossed = feat(crossing, COLUMN)
        parts[i].in_kept = pick(far_in, named(i, 2), block)
        done(crossing, parts[i].in_kept)

    def in3(i):
        kept, crossed = gate(kinds[NEAR][i].kept, kinds[NEAR][i].crossed)
        rows = stack(kept, crossed)
        kinds[NEAR][i].rows = rows
        kinds[NEAR][i].rows_other = other_core(rows)
        done(rows)

    def in4(i):
        out_end, out_mid = gate(parts[i].out_end, parts[i].out_mid)
        if i == 0:
            parts[1].near = feat(gate(parts[1].own), NEIGHBOUR)
        far_out = jnp.where(inner, out_mid, out_end)
        crossing = pick(far_out, named(i, 3), sibling)
        parts[i].out_crossed = feat(crossing, COLUMN)
        parts[i].out_kept = pick(far_out, named(i, 3), block)
        done(crossing, parts[i].out_kept)

    def in5(i):
        rows = stack(*gate(parts[i].in_kept, parts[i].out_kept, parts[i].in_crossed, parts[i].out_crossed))
        kinds[FAR][i].rows = rows
        kinds[FAR][i].rows_other = other_core(rows)
        done(rows)

    def sums(kind):
        def step(i):
            own, other = gate(kinds[kind][i].rows, kinds[kind][i].rows_other)
            upper, lower = rebuild(core_at, own, other, decoder)
            kinds[kind][i].rows, kinds[kind][i].rows_other = own, other
            kinds[kind][i].upper = upper
            kinds[kind][i].lower = feat(lower, COLUMN)
            done(upper, lower)

        return step

    def err1(kind):
        def step(i):
            total = add(*gate(kinds[kind][i].upper, kinds[kind][i].lower))
            first, second = total[: counts[i]], total[counts[i] :]
            keep, send = first, second
            if kind == FAR:
                keep, send = jnp.where(inner, first, second), jnp.where(inner, second, first)
            kinds[kind][i].keep = keep
            kinds[kind][i].sent = feat(send, NEIGHBOUR)
            done(keep, send)

        return step

    def err2(kind):
        def step(i):
            rebuilt = add(*gate(kinds[kind][i].keep, kinds[kind][i].sent))
            grad = error(rebuilt, gate(kinds[kind][i].aim))
            kinds[kind][i].rebuilt = rebuilt
            kinds[kind][i].grad = grad
            kinds[kind][i].grad_sent = feat(grad, NEIGHBOUR)
            done(grad)

        return step

    def err3(kind):
        def step(i):
            grad, sent = gate(kinds[kind][i].grad, kinds[kind][i].grad_sent)
            if kind == FAR:
                grad, sent = jnp.where(inner, grad, sent), jnp.where(inner, sent, grad)
            grads = stack(grad, sent)
            kinds[kind][i].grads = grads
            kinds[kind][i].grads_other = feat(grads, COLUMN)
            done(grads)

        return step

    def terms(kind):
        def step(i):
            upper, lower = gate(kinds[kind][i].grads, kinds[kind][i].grads_other)
            give, keep = code_terms(core_at, upper, lower, decoder)
            kinds[kind][i].grads, kinds[kind][i].grads_other = upper, lower
            kinds[kind][i].terms = keep
            kinds[kind][i].given = other_core(give)
            done(keep, give)

        return step

    def out1(kind):
        def step(i):
            total = add(*gate(kinds[kind][i].terms, kinds[kind][i].given))
            n = counts[i]
            kinds[kind][i].heres[0], kinds[kind][i].heres[1] = total[:n], total[n : 2 * n]
            kinds[kind][i].waits[0] = total[2 * n : 3 * n]
            kinds[kind][i].theres[1] = feat(total[3 * n :], COLUMN)
            done(total)

        return step

    def out1b(kind):
        def step(i):
            give = gate(kinds[kind][i].waits[0])
            kinds[kind][i].theres[0] = feat(give, COLUMN)
            done(give)

        return step

    def out2(kind, slot):
        def step(i):
            here, there = gate(kinds[kind][i].heres[slot], kinds[kind][i].theres[slot])
            name = named(i, slot + 2 * kind)
            out = jnp.stack(
                [
                    jnp.where(
                        name[:, k : k + 1] == block,
                        here,
                        jnp.where(name[:, k : k + 1] == sibling, there, 0),
                    )
                    for k in range(per_token)
                ]
            )
            kinds[kind][i].ys[slot] = out
            if kind == FAR:
                sent = feat(out, INWARD)
                if slot:
                    parts[i].out_sent = sent
                else:
                    parts[i].in_sent = sent
            done(out)

        return step

    def out3(i):
        y_out = add(*gate(kinds[FAR][i].ys[1], parts[i].out_sent))
        parts[i].out_sent = feat(y_out, MIDDLE)
        done(y_out)

    def out3b(i):
        y_in = add(*gate(kinds[FAR][i].ys[0], parts[i].in_sent))
        parts[i].in_sent = feat(y_in, MIDDLE)
        done(y_in)

    def out4(i):
        y_near = add(*gate(kinds[NEAR][i].ys[1], parts[i].out_sent))
        kinds[NEAR][i].sent = feat(y_near, NEIGHBOUR)
        done(y_near)

    def out5(i):
        own = add(*gate(kinds[NEAR][i].ys[0], kinds[NEAR][i].sent, parts[i].in_sent))
        parts[i].sum = own
        parts[i].sum_other = other_core(own)
        done(own)

    def out6(i):
        own, other = gate(parts[i].sum, parts[i].sum_other)
        first = core == 0
        whole = jnp.concatenate(
            [jnp.where(first, own, other), jnp.where(first, other, own)], axis=2
        )
        parts[i].code_grad = jnp.swapaxes(whole, 0, 1)
        done(parts[i].code_grad)

    def weights(i):
        base = None
        rows, grads = [], []
        for part in range(2):
            for kind in (NEAR, FAR):
                rows.append((kinds[kind][part].rows_other if i else kinds[kind][part].rows))
                grads += [kinds[kind][part].grads, kinds[kind][part].grads_other]
        rows[0] = gate(rows[0])
        if i:
            base = parts[0].weight_grad
        parts[i].weight_grad = weight_half(1 - core_at if i else core_at, rows, grads, base)
        done(parts[i].weight_grad)

    def recon1(i):
        far = gate(kinds[FAR][i].rebuilt)
        kinds[FAR][i].done = feat(far, MIRROR)
        done(far)

    def recon2(i):
        own = stack(kinds[NEAR][0].rebuilt, kinds[NEAR][1].rebuilt)
        far = gate(stack(kinds[FAR][0].done, kinds[FAR][1].done))
        first = target == 0
        parts[0].recon = jnp.stack([jnp.where(first, own, far), jnp.where(first, far, own)], axis=1)
        done(parts[0].recon)

    sums_near, sums_far = sums(NEAR), sums(FAR)
    err1_near, err1_far = err1(NEAR), err1(FAR)
    err2_near, err2_far = err2(NEAR), err2(FAR)
    err3_near, err3_far = err3(NEAR), err3(FAR)
    terms_near, terms_far = terms(NEAR), terms(FAR)
    out1_near, out1_far = out1(NEAR), out1(FAR)
    out1b_near, out1b_far = out1b(NEAR), out1b(FAR)
    out2_mine, out2_next = out2(NEAR, 0), out2(NEAR, 1)
    out2_in, out2_out = out2(FAR, 0), out2(FAR, 1)
    order = (
        (prep, 0), (prep, 1), (ids, 0), (in1, 0), (in1x, 0), (in2, 0), (in3, 0), (sums_near, 0),
        (in4, 0), (in5, 0), (in1, 1), (in1x, 1), (sums_far, 0), (in2, 1), (aims, 0), (in3, 1),
        (err1_far, 0), (sums_near, 1), (in4, 1), (err1_near, 0), (err1_near, 1), (err2_far, 0),
        (aims, 1), (in5, 1), (err3_far, 0), (err2_near, 0), (err2_near, 1), (err3_near, 0),
        (sums_far, 1), (terms_far, 0), (err3_near, 1), (err1_far, 1), (out1_far, 0),
        (err2_far, 1), (recon1, 0), (err3_far, 1), (out1b_far, 0), (out2_out, 0), (terms_far, 1),
        (out2_in, 0), (out3, 0), (recon1, 1), (out1_far, 1), (terms_near, 0), (out2_out, 1),
        (out1_near, 0), (out3b, 0), (out1b_far, 1), (terms_near, 1), (out2_next, 0), (out4, 0),
        (out2_in, 1), (out3, 1), (out1_near, 1), (out1b_near, 0), (out1b_near, 1), (weights, 0),
        (out2_mine, 0), (out5, 0), (out3b, 1), (out2_next, 1), (out4, 1), (weights, 1),
        (out6, 0), (recon2, 0), (out2_mine, 1), (out5, 1), (out6, 1),
    )
    for step, i in order:
        step(i)
    code_grad = stack(parts[0].code_grad, parts[1].code_grad)
    return parts[0].recon, code_grad, parts[1].weight_grad


def solution(mesh):
    owners = mesh.shape["feat"]
    plan = dense if owners // PAIRS == 4 and mesh.shape["pair"] == 2 else slotted
    return jax.shard_map(
        plan,
        mesh=mesh,
        in_specs=(
            P(("groups", "feat"), None, None),
            P(("groups", "feat"), None),
            P("feat", "pair"),
            P(("groups", "feat"), None, "pair"),
        ),
        out_specs=(
            P(("groups", "feat"), None, "pair"),
            P(("groups", "feat"), None, None),
            P(("groups", "feat"), "pair"),
        ),
        check_vma=False,
    )
```
